128 devices in a mesh: kb: 16 (over z, x), men: 8 (over y, core).
Axes of the slice: x: 4, y: 4, z: 4, core: 2. Of those that a mesh axis runs over, the one named last changes fastest.
Arguments:
- mentions: bfloat16 [2048, 1024], P('men'), may hold values from -6 to 6
- kb_embed: bfloat16 [65536, 1024], P('kb'), may hold values from -0.1875 to 0.1875
- blocks: bfloat16 [2048, 96, 1024], P(('kb', 'men')), may hold values from -6 to 6
- task_mention: int32 [2048], P(('kb', 'men')), may hold values from 0 to 255
- task_owner: int32 [2048, 1], P(('kb', 'men')), may hold values from 0 to 7, as said below
- task_count: int32 [128], P(('kb', 'men')), may hold values from 1 to 16, as said below
- w_in: bfloat16 [4096, 1024], P('kb'), may hold values from -0.1875 to 0.1875
- w_out: bfloat16 [4096, 1024], P('kb'), may hold values from -0.09375 to 0.09375
- head: bfloat16 [1024], replicated, may hold values from -0.1875 to 0.1875
Outputs:
- best_scores: float32 [2048, 32], P('men')
- owned_scores: float32 [128, 16], P(('kb', 'men'))
The draws below stay inside these ranges and needn't reach their ends.
Inputs may be any that keep to these rules, and one draw needn't show every extreme that they name: `task_owner`: only live slots are routed. At most 2 live tasks of one device share an owner, and some device of every kb index sends exactly 2 to every owner; every owner receives exactly 8 live tasks from the devices of its kb index. `task_count`: in each kb index the counts of the 8 men indices sum to 64; one of them is exactly 16 and one exactly 1.
All inputs are finite; a program needn't handle non-finite values.
Results may differ from the reference program's by a relative error of at most 0.00071.
Values may be sent and summed in bfloat16 or wider, within the bound.
A program may use at most 128 MiB of HBM per device.

```python
import jax
import jax.numpy as jnp
from jax import lax

D = 1024
FF = 4096
K = 32
LEN = 96
MEN_DEV = 256
TASK_DEV = 16
CAP = 2
NKB = 65536
NMEN = 2048
TASKS = 2048
N_KB = 16
N_MEN = 8


def counts_table(key):
    key = jax.random.fold_in(key, 17)
    key_moves, key_order = jax.random.split(key)
    middle = N_MEN - 2
    spare = TASK_DEV * (N_MEN // 2 - 1) - 1
    spread = spare // middle + (jnp.arange(middle, dtype=jnp.int32) < spare % middle).astype(jnp.int32)
    spread = jnp.broadcast_to(spread[None, :], (N_KB, middle)).astype(jnp.int32)
    column = jnp.arange(middle, dtype=jnp.int32)[None, :]
    for move_index in range(2 * middle):
        key_a, key_b, key_c = jax.random.split(jax.random.fold_in(key_moves, move_index), 3)
        source = jax.random.randint(key_a, (N_KB,), 0, middle, dtype=jnp.int32)
        target = (source + jax.random.randint(key_b, (N_KB,), 1, middle, dtype=jnp.int32)) % middle
        have_source = jnp.sum(jnp.where(column == source[:, None], spread, 0), axis=1)
        have_target = jnp.sum(jnp.where(column == target[:, None], spread, 0), axis=1)
        room = jnp.minimum(have_source - 1, TASK_DEV - have_target)
        amount = jax.random.randint(key_c, (N_KB,), 0, room + 1, dtype=jnp.int32)
        spread = spread - jnp.where(column == source[:, None], amount[:, None], 0)
        spread = spread + jnp.where(column == target[:, None], amount[:, None], 0)
    fixed = jnp.broadcast_to(jnp.array([TASK_DEV, 1], jnp.int32)[None, :], (N_KB, 2))
    values = jnp.concatenate([fixed, spread], axis=1)

    def shuffle(row_key):
        return jax.random.permutation(row_key, N_MEN)
    order = jax.vmap(shuffle)(jax.random.split(key_order, N_KB)).astype(jnp.int32)
    return jnp.take_along_axis(values, order, axis=1)


def draw_task_count(key, part):
    return counts_table(key).reshape(N_KB * N_MEN).astype(jnp.int32)


def draw_task_owner(key, part):
    counts = counts_table(key)
    key = jax.random.fold_in(key, 29)
    key_offset, key_perm = jax.random.split(key)
    before = jnp.cumsum(counts, axis=1) - counts
    queue = before[:, :, None] + jnp.arange(TASK_DEV, dtype=jnp.int32)[None, None, :]
    offset = jax.random.randint(key_offset, (N_KB,), 0, N_MEN, dtype=jnp.int32)

    def shuffle(row_key):
        return jax.random.permutation(row_key, N_MEN)
    order = jax.vmap(shuffle)(jax.random.split(key_perm, N_KB)).astype(jnp.int32)
    cyclic = (queue + offset[:, None, None]) % N_MEN
    table = jnp.broadcast_to(order[:, None, :], (N_KB, N_MEN, N_MEN))
    owners = jnp.take_along_axis(table, cyclic, axis=2)
    return owners.reshape(TASKS, 1).astype(jnp.int32)


def plant(entries, own_key, smallest, top_value):
    spot = [jax.random.randint(jax.random.fold_in(own_key, axis), (), 0, length) for axis, length in enumerate(entries.shape)]
    main_axis = entries.shape.index(max(entries.shape))
    neighbour = spot[:main_axis] + [(spot[main_axis] + 1) % entries.shape[main_axis]] + spot[main_axis + 1:]
    return entries.at[tuple(spot)].set(smallest).at[tuple(neighbour)].set(top_value)


def levels(stream_key, shape, pieces, low, top_value):
    def one(dim, blocks):
        draws = jax.random.uniform(jax.random.fold_in(jax.random.fold_in(stream_key, 6), dim), (blocks,), jnp.float32, low / len(pieces), top_value / len(pieces))
        return jnp.repeat(jnp.exp(draws), shape[dim] // blocks).reshape((-1,) + (1,) * (len(shape) - dim - 1))

    factor_of = one(*pieces[0])
    for cut in pieces[1:]:
        factor_of = factor_of * one(*cut)
    return factor_of


def bell_draw(key, dims, deviation, reach, shards=(), kind=jnp.bfloat16):
    result = deviation * jax.random.normal(key, dims, jnp.float32)
    if shards:
        result = result * levels(key, dims, shards, -0.22, 0.18)
    return jnp.clip(result, -reach, reach).astype(kind)


def setup_inputs(seed: int = 0) -> dict:
    seeds = jax.random.split(jax.random.key(seed), 10)
    mentions = bell_draw(seeds[0], (NMEN, D), 1.0, 6.0, ((0, 8),))
    kb_embed = bell_draw(seeds[1], (NKB, D), D ** -0.5, 0.1875, ((0, 16),))
    blocks = bell_draw(seeds[2], (TASKS, LEN, D), 1.0, 6.0, ((0, 128),))
    task_mention = plant(jax.random.randint(seeds[3], (TASKS,), 0, MEN_DEV), jax.random.fold_in(seeds[3], 1), 0, MEN_DEV - 1).astype(jnp.int32)
    task_owner = draw_task_owner(jax.random.fold_in(seeds[9], 71), 0)
    task_count = draw_task_count(jax.random.fold_in(seeds[9], 71), 0)
    w_in = bell_draw(seeds[6], (FF, D), D ** -0.5, 0.1875, ((0, 16),))
    w_out = bell_draw(seeds[7], (FF, D), FF ** -0.5, 0.09375, ((0, 16),))
    head = bell_draw(seeds[8], (D,), D ** -0.5, 0.1875)
    return dict(mentions=mentions, kb_embed=kb_embed, blocks=blocks, task_mention=task_mention, task_owner=task_owner, task_count=task_count, w_in=w_in, w_out=w_out, head=head)


def score_pairs(pair_block, w_in, w_out, head):
    flat_rows = pair_block.reshape(-1, D).astype(jnp.float32)
    mean_square = lax.optimization_barrier(jnp.mean(flat_rows * flat_rows, axis=-1, keepdims=True))
    normed = (flat_rows * lax.rsqrt(mean_square + 1e-06)).astype(jnp.bfloat16)
    pre_act = lax.dot_general(normed, w_in, (((1,), (1,)), ((), ())), preferred_element_type=jnp.float32)
    hidden_act = jax.nn.gelu(pre_act, approximate=False).astype(jnp.bfloat16)
    mixed_rows = flat_rows + jnp.dot(hidden_act, w_out, preferred_element_type=jnp.float32)
    final_square = lax.optimization_barrier(jnp.mean(mixed_rows * mixed_rows, axis=-1, keepdims=True))
    final_rows = mixed_rows * lax.rsqrt(final_square + 1e-06)
    pooled_rows = lax.optimization_barrier(jnp.mean(final_rows.reshape(-1, LEN, D), axis=1))
    return lax.optimization_barrier(jnp.sum(pooled_rows * head.astype(jnp.float32), axis=-1))

def reference(mentions, kb_embed, blocks, task_mention, task_owner, task_count, w_in, w_out, head):

    def retrieve(mention_block):
        scored = jnp.dot(mention_block, kb_embed.T, preferred_element_type=jnp.float32)
        return lax.top_k(scored, K)[0]
    best_scores = lax.map(retrieve, mentions.reshape(N_MEN, MEN_DEV, D)).reshape(NMEN, K)
    devices_all = N_KB * N_MEN
    task_index = jnp.arange(TASKS, dtype=jnp.int32)
    device_of = task_index // TASK_DEV
    group_of = device_of % N_MEN
    kb_of = device_of // N_MEN
    slot_of = task_index % TASK_DEV
    live = slot_of < task_count[device_of]
    live_index = jnp.nonzero(live, size=TASKS // 2, fill_value=0)[0].astype(jnp.int32)
    mention_index = (group_of * MEN_DEV + task_mention).astype(jnp.int32)[live_index]
    mention_rows = mentions[mention_index].astype(jnp.float32)
    pair_input = (blocks[live_index].astype(jnp.float32) + mention_rows[:, None, :]).astype(jnp.bfloat16)

    def score_block(pair_block):
        return score_pairs(pair_block, w_in, w_out, head)
    pair_score = lax.map(score_block, pair_input.reshape(devices_all, TASK_DEV // 2, LEN, D)).reshape(TASKS // 2)
    task_owners = task_owner[:, 0].reshape(devices_all, TASK_DEV)
    live_table = live.reshape(devices_all, TASK_DEV)
    slot_index = jnp.arange(TASK_DEV, dtype=jnp.int32)
    same_owner = task_owners[:, :, None] == task_owners[:, None, :]
    earlier = slot_index[None, :] < slot_index[:, None]
    counted = same_owner & earlier[None, :, :] & live_table[:, None, :]
    slot_rank = lax.optimization_barrier(jnp.sum(counted.astype(jnp.int32), axis=2)).reshape(TASKS)
    row_index = (kb_of * N_MEN + task_owner[:, 0]).astype(jnp.int32)[live_index]
    col_index = (group_of * CAP + slot_rank).astype(jnp.int32)[live_index]
    owned_scores = jnp.zeros((devices_all, N_MEN * CAP), jnp.float32).at[row_index, col_index].set(pair_score)
    return (best_scores, owned_scores)
```

```python
import functools

import jax
import jax.numpy as jnp
from jax import lax
from jax.experimental import pallas as pl
from jax.experimental.pallas import tpu as pltpu
from jax.sharding import PartitionSpec as P

K = 32
LEN = 96
MESH = pl.DeviceIdType.MESH
NT = (((1,), (1,)), ((), ()))
F32 = jnp.float32
BF16 = jnp.bfloat16
RING = 4

ITEMS = [
    (0, 0), (-1, 0), (1, 0), (0, -1), (0, 1), (2, 0), (-1, -1), (-1, 1),
    (1, -1), (1, 1), (0, 2), (2, -1), (2, 1), (-1, 2), (1, 2), (2, 2),
]
SLOT = {item: slot for slot, item in enumerate(ITEMS)}


def wrap(offset):
    return (offset + 1) % RING - 1


def hops(item):
    first, second = item
    if item == (0, 0):
        return [(axis, way, mat) for mat in (0, 1) for axis in "PQ" for way in (1, -1)]
    out = []
    if second == 0:
        if first == -1:
            out.append(("P", 1, 0))
        if first == 1:
            out.append(("P", -1, 1))
        out += [("Q", way, mat) for mat in (0, 1) for way in (1, -1)]
    elif second == -1:
        out.append(("Q", 1, 0))
    elif second == 1:
        out.append(("Q", -1, 1))
    return out


SENDS = []
for item in ITEMS:
    for axis, way, mat in hops(item):
        goal = (wrap(item[0] - way), item[1]) if axis == "P" else (item[0], wrap(item[1] - way))
        SENDS.append((SLOT[item], axis, way, mat, SLOT[goal]))


def sort_pairs(count):
    pairs = []
    p = 1
    while p < count:
        k = p
        while k >= 1:
            for j in range(k % p, count - k, 2 * k):
                for i in range(min(k, count - j - k)):
                    if (i + j) // (2 * p) == (i + j + k) // (2 * p):
                        pairs.append((i + j, i + j + k))
            k //= 2
        p *= 2
    return pairs


PAIRS = sort_pairs(K)


def sort_down(rows):
    rows = list(rows)
    for i, j in PAIRS:
        rows[i], rows[j] = jnp.maximum(rows[i], rows[j]), jnp.minimum(rows[i], rows[j])
    return rows


def merge_down(left, right):
    rows = [jnp.maximum(left[i], right[K - 1 - i]) for i in range(K)]
    stride = K // 2
    while stride:
        for i in range(K):
            if not i & stride:
                rows[i], rows[i + stride] = (
                    jnp.maximum(rows[i], rows[i + stride]),
                    jnp.minimum(rows[i], rows[i + stride]),
                )
        stride //= 2
    return rows


def gelu(x):
    half = 0.5 * x
    return half + half * lax.erf(x * 0.7071067811865476)


CHUNK = 512
TILE = 512
STEPS = [(0, 4), (4, 8), (8, 12), (12, 16)]


def kernel(
    mentions_ref, kb_ref, blocks_ref, pick_ref, owner_ref, count_ref, w_in_ref, w_out_ref, head_ref,
    best_ref, owned_ref,
    rows, total, w_in, w_out, entities, scores, top, mention_rows, lists, lists_in, placed, placed_in,
    send, recv, cross_send, cross_recv, local_sem, kb_sem, list_send, list_recv, place_send, place_recv,
):
    kb = lax.axis_index("kb")
    men = lax.axis_index("men")
    core = lax.rem(men, 2)
    z, x = kb // RING, lax.rem(kb, RING)
    partner = men + 1 - 2 * core

    def along(axis, way):
        step = way % RING
        dz = step * (1 - core) if axis == "P" else step * core
        dx = step * core if axis == "P" else step * (1 - core)
        return lax.rem(z + dz, RING) * RING + lax.rem(x + dx, RING)

    near = {(axis, way): along(axis, way) for axis in "PQ" for way in (1, -1)}
    mine = pl.ds(pl.multiple_of(core * 128, 128), 128)
    weights, shards = (w_in, w_out), (w_in_ref, w_out_ref)

    barrier = pltpu.get_barrier_semaphore()
    for axis in "PQ":
        for way in (1, 2, 3):
            pl.semaphore_signal(barrier, inc=1, device_id=(along(axis, way), men), device_id_type=MESH)
    for way in range(1, 8):
        pl.semaphore_signal(barrier, inc=1, device_id=(kb, lax.rem(men + way, 8)), device_id_type=MESH)

    local = [pltpu.make_async_copy(shards[m], weights[m].at[0], local_sem.at[m]) for m in (0, 1)]
    local.append(pltpu.make_async_copy(blocks_ref, rows, local_sem.at[2]))

    def entity_copy(i, slot):
        return pltpu.make_async_copy(
            kb_ref.at[pl.ds(pl.multiple_of(i * CHUNK, CHUNK), CHUNK)], entities.at[slot], kb_sem.at[slot]
        )

    entity_copy(0, 0).start()
    entity_copy(1, 1).start()
    for copy in local:
        copy.start()

    pl.semaphore_wait(barrier, 13)

    def hop(n):
        slot, axis, way, m, goal = SENDS[n]
        source = shards[m].at[mine] if slot == 0 else weights[m].at[slot, mine]
        return pltpu.make_async_remote_copy(
            src_ref=source, dst_ref=weights[m].at[goal, mine], send_sem=send.at[n], recv_sem=recv.at[goal, m],
            device_id=(near[axis, way], men), device_id_type=MESH,
        )

    def cross(slot, m, half):
        return pltpu.make_async_remote_copy(
            src_ref=weights[m].at[slot, half], dst_ref=weights[m].at[slot, half],
            send_sem=cross_send.at[slot, m], recv_sem=cross_recv.at[slot, m],
            device_id=(kb, partner), device_id_type=MESH,
        )

    def arrived(slot, m):
        pltpu.make_async_remote_copy(
            src_ref=weights[m].at[slot, mine], dst_ref=weights[m].at[slot, mine],
            send_sem=cross_send.at[slot, m], recv_sem=recv.at[slot, m],
            device_id=(kb, partner), device_id_type=MESH,
        ).wait_recv()

    def pass_on(slot):
        for m in (0, 1):
            if slot:
                arrived(slot, m)
            for n, entry in enumerate(SENDS):
                if entry[0] == slot and entry[3] == m:
                    hop(n).start()
            if slot:
                cross(slot, m, mine).start()

    def crossed(slot):
        for m in (0, 1):
            cross(slot, m, mine).wait_recv()

    pass_on(0)

    top[...] = jnp.full(top.shape, -jnp.inf, F32)
    scores[1] = jnp.full(scores.shape[1:], -jnp.inf, F32)
    chunks = kb_ref.shape[0] // CHUNK

    def keep_top(slot):
        for lane in range(2):
            held = [top[lane, i] for i in range(K)]
            for part in range(CHUNK // 256):
                fresh = [
                    scores[slot, part * 256 + i * 8 : part * 256 + i * 8 + 8, lane * 128 : lane * 128 + 128]
                    for i in range(K)
                ]
                held = merge_down(held, sort_down(fresh))
            for i in range(K):
                top[lane, i] = held[i]

    def retrieve(i, carry):
        now = lax.rem(i, 2)
        entity_copy(i, now).wait()
        keep_top(1 - now)
        scores[now] = lax.dot_general(entities[now], mentions_ref[...], NT, preferred_element_type=F32)

        @pl.when(i + 2 < chunks)
        def _():
            entity_copy(i + 2, now).start()

        return carry

    lax.fori_loop(0, chunks, retrieve, 0)
    keep_top((chunks - 1) % 2)

    def list_copy(stage, way):
        axis = "PQ"[stage]
        return pltpu.make_async_remote_copy(
            src_ref=lists.at[stage], dst_ref=lists_in.at[stage, way - 1],
            send_sem=list_send.at[stage, way - 1], recv_sem=list_recv.at[stage, way - 1],
            device_id=(along(axis, way), men), device_id_type=MESH,
        )

    held_lists = []
    for lane in range(2):
        held = [top[lane, i] for i in range(K)]
        for shift in (4, 2, 1):
            held = merge_down(held, [pltpu.roll(row, shift, 0) for row in held])
        for i in range(K):
            top[lane, i] = held[i]
            lists[0, i : i + 1, lane * 128 : lane * 128 + 128] = held[i][0:1]
    for way in (1, 2, 3):
        list_copy(0, way).start()

    slot_col = lax.broadcasted_iota(jnp.int32, (16, 128), 0)
    pick = jnp.zeros((16, 128), jnp.int32)
    for t in range(16):
        pick = jnp.where(slot_col == t, pick_ref[t], pick)
    one_hot = (
        jnp.concatenate([pick, pick], axis=1) == lax.broadcasted_iota(jnp.int32, (16, 256), 1)
    ).astype(F32).astype(BF16)
    mention_rows[...] = jnp.dot(one_hot, mentions_ref[...], preferred_element_type=F32)
    local[2].wait()

    def prepare(t, carry):
        part = pl.ds(pl.multiple_of(t * LEN, LEN), LEN)
        pair = (rows[part, :].astype(F32) + mention_rows[pl.ds(t, 1), :]).astype(BF16).astype(F32)
        square = jnp.mean(pair * pair, axis=1, keepdims=True)
        rows[part, :] = (pair * lax.rsqrt(square + 1e-06)).astype(BF16)
        total[part, :] = pair
        return carry

    lax.fori_loop(0, 16, prepare, 0)
    local[0].wait()
    local[1].wait()

    def merge_lists(stage):
        for way in (1, 2, 3):
            list_copy(stage, way).wait_recv()
        for lane in range(2):
            span = slice(lane * 128, lane * 128 + 128)
            held = [top[lane, i] for i in range(K)]
            for way in range(3):
                held = merge_down(
                    held, [jnp.broadcast_to(lists_in[stage, way, i : i + 1, span], (8, 128)) for i in range(K)]
                )
            for i in range(K):
                if stage == 0:
                    top[lane, i] = held[i]
                    lists[1, i : i + 1, span] = held[i][0:1]
                else:
                    best_ref[i : i + 1, span] = held[i][0:1]

    tiles = rows.shape[0] // TILE
    seen = 0
    for step, (low, high) in enumerate(STEPS):
        while seen < high - 1:
            seen += 1
            pass_on(seen)
        for slot in range(max(low, 1), high):
            crossed(slot)
        width = (high - low) * 256

        def feed(tile, carry, low=low, high=high, width=width):
            part = pl.ds(pl.multiple_of(tile * TILE, TILE), TILE)
            pre = lax.dot_general(
                rows[part, :], w_in[low:high].reshape(width, 1024), NT, preferred_element_type=F32
            )
            act = gelu(pre).astype(BF16)
            total[part, :] += jnp.dot(act, w_out[low:high].reshape(width, 1024), preferred_element_type=F32)
            return carry

        lax.fori_loop(0, tiles, feed, 0)
        if step == 0:
            merge_lists(0)
            for way in (1, 2, 3):
                list_copy(1, way).start()
        if step == 1:
            merge_lists(1)

    head = head_ref[...].astype(F32)

    def score(t, carry):
        part = pl.ds(pl.multiple_of(t * LEN, LEN), LEN)
        mixed = total[part, :]
        square = jnp.mean(mixed * mixed, axis=1, keepdims=True)
        dots = jnp.sum(mixed * head, axis=1, keepdims=True)
        value = jnp.sum(dots * lax.rsqrt(square + 1e-06), axis=0, keepdims=True) * (1.0 / LEN)
        return jnp.where(slot_col == t, jnp.broadcast_to(value, (16, 128)), carry)

    pair_score = lax.fori_loop(0, 16, score, jnp.zeros((16, 128), F32))
    live = count_ref[0]
    owner = jnp.zeros((16, 128), jnp.int32)
    for t in range(16):
        owner = jnp.where(slot_col == t, owner_ref[t, 0], owner)
    rank = jnp.zeros((16, 128), jnp.int32)
    for s in range(16):
        same = (slot_col > s) & (owner == owner_ref[s, 0]) & (jnp.full((16, 128), s, jnp.int32) < live)
        rank = rank + jnp.where(same, 1, 0)
    lane_id = lax.broadcasted_iota(jnp.int32, (16, 128), 1)
    base = jnp.where((lane_id == men * 2 + rank) & (slot_col < live), pair_score, 0.0)
    for o in range(8):
        line = jnp.sum(jnp.where(owner == o, base, 0.0), axis=0, keepdims=True)
        placed[o] = jnp.broadcast_to(line, (8, 128))

    def place_copy(way):
        goal = lax.rem(men + way, 8)
        return pltpu.make_async_remote_copy(
            src_ref=placed.at[goal], dst_ref=placed_in.at[way - 1],
            send_sem=place_send.at[way - 1], recv_sem=place_recv.at[way - 1],
            device_id=(kb, goal), device_id_type=MESH,
        )

    for way in range(1, 8):
        place_copy(way).start()
    owned = placed[men]
    for n in range(len(SENDS)):
        hop(n).wait_send()
    for slot in range(1, 16):
        for m in (0, 1):
            cross(slot, m, mine).wait_send()
    for stage in (0, 1):
        for way in (1, 2, 3):
            list_copy(stage, way).wait_send()
    for way in range(1, 8):
        place_copy(way).wait()
        owned = owned + placed_in[way - 1]
    owned_ref[...] = owned


def body(mentions, kb_embed, blocks, task_mention, task_owner, task_count, w_in, w_out, head):
    width = mentions.shape[1]
    token_rows = blocks.shape[0] * blocks.shape[1]
    group = mentions.shape[0]
    anywhere = pl.BlockSpec(memory_space=pl.ANY)
    vmem = pl.BlockSpec(memory_space=pltpu.VMEM)
    smem = pl.BlockSpec(memory_space=pltpu.SMEM)
    dma = pltpu.SemaphoreType.DMA
    best, owned = pl.pallas_call(
        kernel,
        out_shape=(jax.ShapeDtypeStruct((K, group), F32), jax.ShapeDtypeStruct((8, 128), F32)),
        in_specs=[vmem, anywhere, anywhere, smem, smem, smem, anywhere, anywhere, vmem],
        out_specs=(vmem, vmem),
        scratch_shapes=[
            pltpu.VMEM((token_rows, width), BF16),
            pltpu.VMEM((token_rows, width), F32),
            pltpu.VMEM((16, 256, width), BF16),
            pltpu.VMEM((16, 256, width), BF16),
            pltpu.VMEM((2, CHUNK, width), BF16),
            pltpu.VMEM((2, CHUNK, group), F32),
            pltpu.VMEM((2, K, 8, 128), F32),
            pltpu.VMEM((16, width), F32),
            pltpu.VMEM((2, K, group), F32),
            pltpu.VMEM((2, 3, K, group), F32),
            pltpu.VMEM((8, 8, 128), F32),
            pltpu.VMEM((7, 8, 128), F32),
            dma((len(SENDS),)),
            dma((16, 2)),
            dma((16, 2)),
            dma((16, 2)),
            dma((3,)),
            dma((2,)),
            dma((2, 3)),
            dma((2, 3)),
            dma((7,)),
            dma((7,)),
        ],
        compiler_params=pltpu.CompilerParams(
            collective_id=0, has_side_effects=True, vmem_limit_bytes=60 * 1024 * 1024
        ),
        cost_estimate=pl.CostEstimate(flops=28_000_000_000, bytes_accessed=14_000_000, transcendentals=6_300_000),
    )(
        mentions, kb_embed, blocks.reshape(token_rows, width), task_mention, task_owner, task_count,
        w_in, w_out, head.reshape(1, width),
    )
    return best.T, owned[0:1, 0:16]


def solution(mesh):
    in_specs = (
        P("men", None),
        P("kb", None),
        P(("kb", "men"), None, None),
        P(("kb", "men")),
        P(("kb", "men"), None),
        P(("kb", "men")),
        P("kb", None),
        P("kb", None),
        P(),
    )
    out_specs = (P("men", None), P(("kb", "men"), None))
    return jax.shard_map(body, mesh=mesh, in_specs=in_specs, out_specs=out_specs, check_vma=False)
```

```python
import functools

import jax
import jax.numpy as jnp
from jax import lax
from jax.experimental import pallas as pl
from jax.experimental.pallas import tpu as pltpu
from jax.sharding import PartitionSpec as P

K = 32
LEN = 96
MESH = pl.DeviceIdType.MESH
NT = (((1,), (1,)), ((), ()))
F32 = jnp.float32
BF16 = jnp.bfloat16
RING = 4

ITEMS = [
    (0, 0), (-1, 0), (1, 0), (0, -1), (0, 1), (0, 2), (-1, 1), (2, 0),
    (-1, -1), (1, -1), (1, 1), (-1, 2), (2, -1), (2, 1), (1, 2), (2, 2),
]
SLOT = {item: slot for slot, item in enumerate(ITEMS)}
QUARTERED = {SLOT[item] for item in ((0, 1), (0, -1), (0, 2),)}


def wrap(offset):
    return (offset + 1) % RING - 1


def hops(item):
    first, second = item
    if item == (0, 0):
        return [("Q", way, mat) for mat in (0, 1) for way in (1, -1)] + [
            ("P", way, mat) for mat in (0, 1) for way in (1, -1)
        ]
    out = []
    if second == 0:
        if first == -1:
            out.append(("P", 1, 0))
        if first == 1:
            out.append(("P", -1, 1))
        out += [("Q", way, mat) for mat in (0, 1) for way in (1, -1)]
    elif second == -1:
        out.append(("Q", 1, 0))
    elif second == 1:
        out.append(("Q", -1, 1))
    return out


COPIES = []
HOPS, HOPPED, RING_SENDS, RING_PASSES, CROSSES = {}, {}, {}, {}, {}
for item in ITEMS:
    slot = SLOT[item]
    for axis, way, mat in hops(item):
        goal = (wrap(item[0] - way), item[1]) if axis == "P" else (item[0], wrap(item[1] - way))
        HOPS.setdefault((slot, mat), []).append(len(COPIES))
        HOPPED[SLOT[goal], mat] = len(COPIES)
        COPIES.append(("hop", slot, axis, way, mat, SLOT[goal]))
for slot in sorted(QUARTERED):
    for way in (1, -1):
        RING_SENDS[slot, way] = len(COPIES)
        COPIES.append(("ring", slot, way, 0, 2, 0))
        RING_PASSES[slot, way] = len(COPIES)
        COPIES.append(("ring", slot, way, (1 - way) // 2, 1, -way))
    CROSSES[slot, 0] = len(COPIES)
    COPIES.append(("cross", slot, 0, 2))
for slot in range(1, 16):
    if slot not in QUARTERED:
        for mat in (0, 1):
            CROSSES[slot, mat] = len(COPIES)
            COPIES.append(("cross", slot, mat, 1))

EVENTS = {
    ("r", 3): [("L",)],
    ("r", 5): [("A", (0, 1)), ("A", (0, -1))],
    ("p", 0): [("D", (1, 0), 0), ("D", (-1, 0), 0)],
    ("p", 1): [("A", (0, 2))],
    (0, 1): [("D", (-1, 0), 1), ("D", (1, 0), 1)],
    (1, 0): [("B", (0, 1)), ("B", (0, -1))],
    (1, 2): [("B", (0, 2))],
    (2, 0): [("C", (0, -1)), ("C", (0, 1)), ("C", (0, 2))],
    (2, 1): [("D", (1, 1), 0), ("D", (-1, 1), 0)],
    (2, 2): [("D", (-1, -1), 0), ("D", (2, 0), 0), ("D", (1, -1), 0)],
    (3, 0): [("D", (-1, 1), 1), ("D", (2, 0), 1), ("D", (-1, -1), 1), ("D", (1, -1), 1), ("D", (1, 1), 1)],
    (3, 2): [("D", (2, 1), 0)],
    (4, 2): [("D", (-1, 2), 0), ("D", (1, 2), 1), ("D", (2, -1), 1), ("D", (-1, 2), 1), ("D", (2, -1), 0), ("D", (2, 1), 1), ("D", (1, 2), 0)],
    (5, 2): [("D", (2, 2), 1), ("D", (2, 2), 0)],
}


def sort_pairs(count):
    pairs = []
    p = 1
    while p < count:
        k = p
        while k >= 1:
            for j in range(k % p, count - k, 2 * k):
                for i in range(min(k, count - j - k)):
                    if (i + j) // (2 * p) == (i + j + k) // (2 * p):
                        pairs.append((i + j, i + j + k))
            k //= 2
        p *= 2
    return pairs


PAIRS = sort_pairs(K)


def sort_down(rows):
    rows = list(rows)
    for i, j in PAIRS:
        rows[i], rows[j] = jnp.maximum(rows[i], rows[j]), jnp.minimum(rows[i], rows[j])
    return rows


def merge_down(left, right):
    rows = [jnp.maximum(left[i], right[K - 1 - i]) for i in range(K)]
    stride = K // 2
    while stride:
        for i in range(K):
            if not i & stride:
                rows[i], rows[i + stride] = (
                    jnp.maximum(rows[i], rows[i + stride]),
                    jnp.minimum(rows[i], rows[i + stride]),
                )
        stride //= 2
    return rows


def gelu(x):
    half = 0.5 * x
    return half + half * lax.erf(x * 0.7071067811865476)


CHUNK = 512
TILE = 512
LIST_STEP = 3
STEPS = [(0, 1), (1, 3), (3, 5), (5, 9), (9, 11), (11, 15), (15, 16)]


def kernel(
    mentions_ref, kb_ref, blocks_ref, pick_ref, owner_ref, count_ref, w_in_ref, w_out_ref, head_ref,
    best_ref, owned_ref,
    rows, total, weights, entities, scores, top, mention_rows, lists, lists_in, placed, placed_in,
    send, recv, local_sem, kb_sem, list_send, list_recv, place_send, place_recv,
):
    kb = lax.axis_index("kb")
    men = lax.axis_index("men")
    core = lax.rem(men, 2)
    z, x = kb // RING, lax.rem(kb, RING)
    partner = men + 1 - 2 * core
    layer = men // 2

    def along(axis, way):
        step = way % RING
        dz = step * (1 - core) if axis == "P" else step * core
        dx = step * core if axis == "P" else step * (1 - core)
        return lax.rem(z + dz, RING) * RING + lax.rem(x + dx, RING)

    near = {(axis, way): along(axis, way) for axis in "PQ" for way in (1, -1)}
    mine = pl.ds(pl.multiple_of(core * 128, 128), 128)
    shards = (w_in_ref, w_out_ref)

    barrier = pltpu.get_barrier_semaphore()
    for axis in "PQ":
        for way in (1, 2, 3):
            pl.semaphore_signal(barrier, inc=1, device_id=(along(axis, way), men), device_id_type=MESH)
    for way in range(1, 8):
        pl.semaphore_signal(barrier, inc=1, device_id=(kb, lax.rem(men + way, 8)), device_id_type=MESH)

    local = [pltpu.make_async_copy(shards[m], weights.at[0, m], local_sem.at[m]) for m in (0, 1)]
    local.append(pltpu.make_async_copy(blocks_ref, rows, local_sem.at[2]))

    def entity_copy(i, slot):
        return pltpu.make_async_copy(
            kb_ref.at[pl.ds(pl.multiple_of(i * CHUNK, CHUNK), CHUNK)], entities.at[slot], kb_sem.at[slot]
        )

    entity_copy(0, 0).start()
    entity_copy(1, 1).start()
    for copy in local:
        copy.start()

    pl.semaphore_wait(barrier, 13)

    quarters = {
        way: pl.ds(pl.multiple_of(core * 128 + lax.rem(layer + way % RING, RING) * 32, 32), 32) for way in (-1, 0, 1)
    }
    rings = {way: lax.rem(men + 2 * (way % RING), 8) for way in (1, -1)}

    def copy_of(n):
        kind, slot, *rest = COPIES[n]
        if kind == "hop":
            axis, way, m, goal = rest
            part = quarters[0] if goal in QUARTERED else mine
            source = shards[m].at[part] if slot == 0 else weights.at[slot, m, part]
            target = weights.at[goal, m, part]
            device = (near[axis, way], men)
        elif kind == "ring":
            way, m, count, shift = rest
            source = target = weights.at[slot, pl.ds(m, count), quarters[shift]]
            device = (kb, rings[way])
        else:
            m, count = rest
            source = target = weights.at[slot, pl.ds(m, count), mine]
            device = (kb, partner)
        return pltpu.make_async_remote_copy(
            src_ref=source, dst_ref=target, send_sem=send.at[n], recv_sem=recv.at[n],
            device_id=device, device_id_type=MESH,
        )

    def start(n):
        copy_of(n).start()

    def arrived(n):
        copy_of(n).wait_recv()

    def handle(event):
        if event[0] == "L":
            for n in HOPS[0, 1]:
                if COPIES[n][2] == "P":
                    start(n)
            return
        kind, item = event[:2]
        slot = SLOT[item]
        if kind == "D":
            m = event[2]
            arrived(HOPPED[slot, m])
            for n in HOPS.get((slot, m), []):
                start(n)
            start(CROSSES[slot, m])
        elif kind == "A":
            for m in (0, 1):
                arrived(HOPPED[slot, m])
                for n in HOPS.get((slot, m), []):
                    start(n)
            for way in (1, -1):
                start(RING_SENDS[slot, way])
        elif kind == "B":
            for way in (1, -1):
                arrived(RING_SENDS[slot, way])
                start(RING_PASSES[slot, way])
        else:
            for way in (1, -1):
                arrived(RING_PASSES[slot, way])
            start(CROSSES[slot, 0])

    def handle_all(*place):
        for event in EVENTS.get(place, []):
            handle(event)

    for m in (0, 1):
        for n in HOPS[0, m]:
            if COPIES[n][2] == "Q":
                start(n)
    for m in (0, 1):
        for n in HOPS[0, m]:
            if COPIES[n][2] == "P" and m == 0:
                start(n)

    top[...] = jnp.full(top.shape, -jnp.inf, F32)
    scores[1] = jnp.full(scores.shape[1:], -jnp.inf, F32)
    chunks = kb_ref.shape[0] // CHUNK

    def keep_top(slot):
        for lane in range(2):
            held = [top[lane, i] for i in range(K)]
            for part in range(CHUNK // 256):
                fresh = [
                    scores[slot, part * 256 + i * 8 : part * 256 + i * 8 + 8, lane * 128 : lane * 128 + 128]
                    for i in range(K)
                ]
                held = merge_down(held, sort_down(fresh))
            for i in range(K):
                top[lane, i] = held[i]

    def retrieve(i, carry):
        now = lax.rem(i, 2)
        entity_copy(i, now).wait()
        keep_top(1 - now)
        scores[now] = lax.dot_general(entities[now], mentions_ref[...], NT, preferred_element_type=F32)

        for place in range(chunks):
            if ("r", place) in EVENTS:

                @pl.when(i == place)
                def _(place=place):
                    handle_all("r", place)

        @pl.when(i + 2 < chunks)
        def _():
            entity_copy(i + 2, now).start()

        return carry

    lax.fori_loop(0, chunks, retrieve, 0)
    keep_top((chunks - 1) % 2)

    def list_copy(stage, way):
        axis = "PQ"[stage]
        return pltpu.make_async_remote_copy(
            src_ref=lists.at[stage], dst_ref=lists_in.at[stage, way - 1],
            send_sem=list_send.at[stage, way - 1], recv_sem=list_recv.at[stage, way - 1],
            device_id=(along(axis, way), men), device_id_type=MESH,
        )

    for lane in range(2):
        held = [top[lane, i] for i in range(K)]
        for shift in (4, 2, 1):
            held = merge_down(held, [pltpu.roll(row, shift, 0) for row in held])
        for i in range(K):
            top[lane, i] = held[i]
            lists[0, i : i + 1, lane * 128 : lane * 128 + 128] = held[i][0:1]
    for way in (1, 2, 3):
        list_copy(0, way).start()

    handle_all("m", 0)

    slot_col = lax.broadcasted_iota(jnp.int32, (16, 128), 0)
    pick = jnp.zeros((16, 128), jnp.int32)
    for t in range(16):
        pick = jnp.where(slot_col == t, pick_ref[t], pick)
    one_hot = (
        jnp.concatenate([pick, pick], axis=1) == lax.broadcasted_iota(jnp.int32, (16, 256), 1)
    ).astype(F32).astype(BF16)
    mention_rows[...] = jnp.dot(one_hot, mentions_ref[...], preferred_element_type=F32)
    local[2].wait()

    def prepare(t, carry):
        part = pl.ds(pl.multiple_of(t * LEN, LEN), LEN)
        pair = (rows[part, :].astype(F32) + mention_rows[pl.ds(t, 1), :]).astype(BF16).astype(F32)
        square = jnp.mean(pair * pair, axis=1, keepdims=True)
        rows[part, :] = (pair * lax.rsqrt(square + 1e-06)).astype(BF16)
        total[part, :] = pair
        return carry

    for part in (0, 1):
        lax.fori_loop(part * 8, part * 8 + 8, prepare, 0)
        handle_all("p", part)
    local[0].wait()
    local[1].wait()

    def merge_lists(stage):
        for way in (1, 2, 3):
            list_copy(stage, way).wait_recv()
        for lane in range(2):
            span = slice(lane * 128, lane * 128 + 128)
            held = [top[lane, i] for i in range(K)]
            for way in range(3):
                held = merge_down(
                    held, [jnp.broadcast_to(lists_in[stage, way, i : i + 1, span], (8, 128)) for i in range(K)]
                )
            for i in range(K):
                if stage == 0:
                    top[lane, i] = held[i]
                    lists[1, i : i + 1, span] = held[i][0:1]
                else:
                    best_ref[i : i + 1, span] = held[i][0:1]

    tiles = rows.shape[0] // TILE
    for step, (low, high) in enumerate(STEPS):
        handle_all(step, 0)
        for slot in range(max(low, 1), high):
            for m in (0, 1):
                if (slot, m) in CROSSES:
                    arrived(CROSSES[slot, m])
        width = (high - low) * 256

        def feed(tile, carry, step=step, low=low, high=high, width=width):
            for place in (1, 2):
                if (step, place) in EVENTS:

                    @pl.when(tile == place)
                    def _(place=place):
                        handle_all(step, place)

            part = pl.ds(pl.multiple_of(tile * TILE, TILE), TILE)
            pre = lax.dot_general(
                rows[part, :], weights[low:high, 0].reshape(width, 1024), NT, preferred_element_type=F32
            )
            act = gelu(pre).astype(BF16)
            total[part, :] += jnp.dot(act, weights[low:high, 1].reshape(width, 1024), preferred_element_type=F32)
            return carry

        lax.fori_loop(0, tiles, feed, 0)
        if step == LIST_STEP:
            merge_lists(0)
            for way in (1, 2, 3):
                list_copy(1, way).start()

    head = head_ref[...].astype(F32).reshape(1, -1)

    def score(t, carry):
        part = pl.ds(pl.multiple_of(t * LEN, LEN), LEN)
        mixed = total[part, :]
        square = jnp.mean(mixed * mixed, axis=1, keepdims=True)
        dots = jnp.sum(mixed * head, axis=1, keepdims=True)
        value = jnp.sum(dots * lax.rsqrt(square + 1e-06), axis=0, keepdims=True) * (1.0 / LEN)
        return jnp.where(slot_col == t, jnp.broadcast_to(value, (16, 128)), carry)

    pair_score = lax.fori_loop(0, 16, score, jnp.zeros((16, 128), F32))
    live = count_ref[0]
    owner = jnp.zeros((16, 128), jnp.int32)
    for t in range(16):
        owner = jnp.where(slot_col == t, owner_ref[t], owner)
    rank = jnp.zeros((16, 128), jnp.int32)
    for s in range(16):
        same = (slot_col > s) & (owner == owner_ref[s]) & (jnp.full((16, 128), s, jnp.int32) < live)
        rank = rank + jnp.where(same, 1, 0)
    lane_id = lax.broadcasted_iota(jnp.int32, (16, 128), 1)
    base = jnp.where((lane_id == men * 2 + rank) & (slot_col < live), pair_score, 0.0)
    for o in range(8):
        line = jnp.sum(jnp.where(owner == o, base, 0.0), axis=0, keepdims=True)
        placed[o] = jnp.broadcast_to(line, (8, 128))

    def place_copy(way):
        goal = lax.rem(men + way, 8)
        return pltpu.make_async_remote_copy(
            src_ref=placed.at[goal], dst_ref=placed_in.at[way - 1],
            send_sem=place_send.at[way - 1], recv_sem=place_recv.at[way - 1],
            device_id=(kb, goal), device_id_type=MESH,
        )

    for way in range(1, 8):
        place_copy(way).start()
    merge_lists(1)
    owned = placed[men]
    for n in range(len(COPIES)):
        copy_of(n).wait_send()
    for stage in (0, 1):
        for way in (1, 2, 3):
            list_copy(stage, way).wait_send()
    for way in range(1, 8):
        place_copy(way).wait()
        owned = owned + placed_in[way - 1]
    owned_ref[...] = owned


def body(mentions, kb_embed, blocks, task_mention, task_owner, task_count, w_in, w_out, head):
    width = mentions.shape[1]
    token_rows = blocks.shape[0] * blocks.shape[1]
    group = mentions.shape[0]
    anywhere = pl.BlockSpec(memory_space=pl.ANY)
    vmem = pl.BlockSpec(memory_space=pltpu.VMEM)
    smem = pl.BlockSpec(memory_space=pltpu.SMEM)
    dma = pltpu.SemaphoreType.DMA
    best, owned = pl.pallas_call(
        kernel,
        out_shape=(jax.ShapeDtypeStruct((K, group), F32), jax.ShapeDtypeStruct((8, 128), F32)),
        in_specs=[vmem, anywhere, anywhere, smem, smem, smem, anywhere, anywhere, vmem],
        out_specs=(vmem, vmem),
        scratch_shapes=[
            pltpu.VMEM((token_rows, width), BF16),
            pltpu.VMEM((token_rows, width), F32),
            pltpu.VMEM((16, 2, 256, width), BF16),
            pltpu.VMEM((2, CHUNK, width), BF16),
            pltpu.VMEM((2, CHUNK, group), F32),
            pltpu.VMEM((2, K, 8, 128), F32),
            pltpu.VMEM((16, width), F32),
            pltpu.VMEM((2, K, group), F32),
            pltpu.VMEM((2, 3, K, group), F32),
            pltpu.VMEM((8, 8, 128), F32),
            pltpu.VMEM((7, 8, 128), F32),
            dma((len(COPIES),)),
            dma((len(COPIES),)),
            dma((3,)),
            dma((2,)),
            dma((2, 3)),
            dma((2, 3)),
            dma((7,)),
            dma((7,)),
        ],
        compiler_params=pltpu.CompilerParams(
            collective_id=0, has_side_effects=True, vmem_limit_bytes=60 * 1024 * 1024
        ),
        cost_estimate=pl.CostEstimate(flops=28_000_000_000, bytes_accessed=14_000_000, transcendentals=6_300_000),
    )(
        mentions, kb_embed, blocks.reshape(token_rows, width), task_mention, task_owner.reshape(-1), task_count,
        w_in, w_out, head,
    )
    return best.T, owned[0:1, 0:16]


def solution(mesh):
    in_specs = (
        P("men", None),
        P("kb", None),
        P(("kb", "men"), None, None),
        P(("kb", "men")),
        P(("kb", "men"), None),
        P(("kb", "men")),
        P("kb", None),
        P("kb", None),
        P(),
    )
    out_specs = (P("men", None), P(("kb", "men"), None))
    return jax.shard_map(body, mesh=mesh, in_specs=in_specs, out_specs=out_specs, check_vma=False)
```

```python
import functools

import jax
import jax.numpy as jnp
from jax import lax
from jax.experimental import pallas as pl
from jax.experimental.pallas import tpu as pltpu
from jax.sharding import PartitionSpec as P

K = 32
LEN = 96
MESH = pl.DeviceIdType.MESH
NT = (((1,), (1,)), ((), ()))
F32 = jnp.float32
BF16 = jnp.bfloat16
RING = 4

ITEMS = [
    (0, 0), (-1, 0), (1, 0), (0, -1), (0, 1), (2, 0), (0, 2), (-1, 1),
    (-1, -1), (1, 1), (1, -1), (2, 1), (-1, 2), (1, 2), (2, -1), (2, 2),
]
SLOT = {item: slot for slot, item in enumerate(ITEMS)}
QUARTERED = {SLOT[item] for item in ((0, 1), (0, -1), (0, 2),)}


def wrap(offset):
    return (offset + 1) % RING - 1


def hops(item):
    first, second = item
    if item == (0, 0):
        return [("Q", way, mat) for mat in (0, 1) for way in (1, -1)] + [
            ("P", way, mat) for mat in (0, 1) for way in (1, -1)
        ]
    out = []
    if second == 0:
        if first == -1:
            out.append(("P", 1, 0))
        if first == 1:
            out.append(("P", -1, 1))
        out += [("Q", way, mat) for mat in (0, 1) for way in (1, -1)]
    elif second == -1:
        out.append(("Q", 1, 0))
    elif second == 1:
        out.append(("Q", -1, 1))
    return out


COPIES = []
HOPS, HOPPED, RING_SENDS, RING_PASSES, CROSSES = {}, {}, {}, {}, {}
for item in ITEMS:
    slot = SLOT[item]
    for axis, way, mat in hops(item):
        goal = (wrap(item[0] - way), item[1]) if axis == "P" else (item[0], wrap(item[1] - way))
        HOPS.setdefault((slot, mat), []).append(len(COPIES))
        HOPPED[SLOT[goal], mat] = len(COPIES)
        COPIES.append(("hop", slot, axis, way, mat, SLOT[goal]))
for slot in sorted(QUARTERED):
    for way in (1, -1):
        RING_SENDS[slot, way] = len(COPIES)
        COPIES.append(("ring", slot, way, 0, 2, 0))
        RING_PASSES[slot, way] = len(COPIES)
        COPIES.append(("ring", slot, way, (1 - way) // 2, 1, -way))
    CROSSES[slot, 0] = len(COPIES)
    COPIES.append(("cross", slot, 0, 2))
for slot in range(1, 16):
    if slot not in QUARTERED:
        for mat in (0, 1):
            CROSSES[slot, mat] = len(COPIES)
            COPIES.append(("cross", slot, mat, 1))

EVENTS = {
    ("r", 0): [("L",)],
    ("r", 7): [("A", (0, -1)), ("A", (0, 1))],
    ("p", 0): [("D", (-1, 0), 0), ("D", (1, 0), 0)],
    (0, 1): [("A", (0, 2)), ("B", (0, -1))],
    (1, 0): [("D", (-1, 0), 1), ("D", (1, 0), 1), ("B", (0, 1)), ("D", (-1, 1), 0)],
    (1, 1): [("D", (-1, -1), 0), ("B", (0, 2))],
    (2, 0): [("D", (2, 0), 0), ("D", (1, 1), 0), ("C", (0, -1)), ("C", (0, 1)), ("D", (1, -1), 0), ("D", (2, 0), 1), ("C", (0, 2))],
    (2, 1): [("D", (-1, 1), 1), ("D", (-1, -1), 1)],
    (3, 0): [("D", (1, 1), 1), ("D", (1, -1), 1)],
    (3, 1): [("D", (2, 1), 0), ("D", (-1, 2), 0)],
    (4, 0): [("D", (2, -1), 0), ("D", (2, 1), 1)],
    (4, 1): [("D", (-1, 2), 1), ("D", (1, 2), 0)],
    (5, 0): [("D", (1, 2), 1), ("D", (2, -1), 1)],
    (5, 1): [("D", (2, 2), 0), ("D", (2, 2), 1)],
}


def sort_pairs(count):
    pairs = []
    p = 1
    while p < count:
        k = p
        while k >= 1:
            for j in range(k % p, count - k, 2 * k):
                for i in range(min(k, count - j - k)):
                    if (i + j) // (2 * p) == (i + j + k) // (2 * p):
                        pairs.append((i + j, i + j + k))
            k //= 2
        p *= 2
    return pairs


PAIRS = sort_pairs(K)


def sort_down(rows):
    rows = list(rows)
    for i, j in PAIRS:
        rows[i], rows[j] = jnp.maximum(rows[i], rows[j]), jnp.minimum(rows[i], rows[j])
    return rows


def merge_down(left, right):
    rows = [jnp.maximum(left[i], right[K - 1 - i]) for i in range(K)]
    stride = K // 2
    while stride:
        for i in range(K):
            if not i & stride:
                rows[i], rows[i + stride] = (
                    jnp.maximum(rows[i], rows[i + stride]),
                    jnp.minimum(rows[i], rows[i + stride]),
                )
        stride //= 2
    return rows


def gelu(x):
    half = 0.5 * x
    return half + half * lax.erf(x * 0.7071067811865476)


CHUNK = 512
LIST_STEP = 3
STEPS = [(0, 1), (1, 3), (3, 5), (5, 9), (9, 11), (11, 13), (13, 16)]


def kernel(
    mentions_ref, kb_ref, blocks_ref, pick_ref, owner_ref, count_ref, w_in_ref, w_out_ref, head_ref,
    best_ref, owned_ref,
    rows, total, weights, entities, scores, top, mention_rows, lists, lists_in, placed, placed_in,
    send, recv, local_sem, kb_sem, list_send, list_recv, place_send, place_recv,
):
    kb = lax.axis_index("kb")
    men = lax.axis_index("men")
    core = lax.rem(men, 2)
    z, x = kb // RING, lax.rem(kb, RING)
    partner = men + 1 - 2 * core
    layer = men // 2

    def along(axis, way):
        step = way % RING
        dz = step * (1 - core) if axis == "P" else step * core
        dx = step * core if axis == "P" else step * (1 - core)
        return lax.rem(z + dz, RING) * RING + lax.rem(x + dx, RING)

    near = {(axis, way): along(axis, way) for axis in "PQ" for way in (1, -1)}
    mine = pl.ds(pl.multiple_of(core * 128, 128), 128)
    shards = (w_in_ref, w_out_ref)

    barrier = pltpu.get_barrier_semaphore()
    for axis in "PQ":
        for way in (1, 2, 3):
            pl.semaphore_signal(barrier, inc=1, device_id=(along(axis, way), men), device_id_type=MESH)
    for way in range(1, 8):
        pl.semaphore_signal(barrier, inc=1, device_id=(kb, lax.rem(men + way, 8)), device_id_type=MESH)

    local = [pltpu.make_async_copy(shards[m], weights.at[0, m], local_sem.at[m]) for m in (0, 1)]
    local.append(pltpu.make_async_copy(blocks_ref, rows, local_sem.at[2]))

    def entity_copy(i):
        return pltpu.make_async_copy(
            kb_ref.at[pl.ds(pl.multiple_of(i * CHUNK, CHUNK), CHUNK)], entities.at[i], kb_sem.at[i]
        )

    chunks = kb_ref.shape[0] // CHUNK
    entity_copy(0).start()
    local[0].start()
    local[1].start()
    for i in range(1, chunks):
        entity_copy(i).start()
    local[2].start()

    slot_col = lax.broadcasted_iota(jnp.int32, (16, 128), 0)
    pick = jnp.zeros((16, 128), jnp.int32)
    for t in range(16):
        pick = jnp.where(slot_col == t, pick_ref[t], pick)
    one_hot = (
        jnp.concatenate([pick, pick], axis=1) == lax.broadcasted_iota(jnp.int32, (16, 256), 1)
    ).astype(F32).astype(BF16)
    mention_rows[...] = jnp.dot(one_hot, mentions_ref[...], preferred_element_type=F32)
    top[...] = jnp.full(top.shape, -jnp.inf, F32)
    scores[1] = jnp.full(scores.shape[1:], -jnp.inf, F32)

    pl.semaphore_wait(barrier, 13)

    quarters = {
        way: pl.ds(pl.multiple_of(core * 128 + lax.rem(layer + way % RING, RING) * 32, 32), 32) for way in (-1, 0, 1)
    }
    rings = {way: lax.rem(men + 2 * (way % RING), 8) for way in (1, -1)}

    def copy_of(n):
        kind, slot, *rest = COPIES[n]
        if kind == "hop":
            axis, way, m, goal = rest
            part = quarters[0] if goal in QUARTERED else mine
            source = shards[m].at[part] if slot == 0 else weights.at[slot, m, part]
            target = weights.at[goal, m, part]
            device = (near[axis, way], men)
        elif kind == "ring":
            way, m, count, shift = rest
            source = target = weights.at[slot, pl.ds(m, count), quarters[shift]]
            device = (kb, rings[way])
        else:
            m, count = rest
            source = target = weights.at[slot, pl.ds(m, count), mine]
            device = (kb, partner)
        return pltpu.make_async_remote_copy(
            src_ref=source, dst_ref=target, send_sem=send.at[n], recv_sem=recv.at[n],
            device_id=device, device_id_type=MESH,
        )

    def start(n):
        copy_of(n).start()

    def arrived(n):
        copy_of(n).wait_recv()

    def handle(event):
        if event[0] == "L":
            for n in HOPS[0, 1]:
                if COPIES[n][2] == "P":
                    start(n)
            return
        kind, item = event[:2]
        slot = SLOT[item]
        if kind == "D":
            m = event[2]
            arrived(HOPPED[slot, m])
            for n in HOPS.get((slot, m), []):
                start(n)
            start(CROSSES[slot, m])
        elif kind == "A":
            for m in (0, 1):
                arrived(HOPPED[slot, m])
                for n in HOPS.get((slot, m), []):
                    start(n)
            for way in (1, -1):
                start(RING_SENDS[slot, way])
        elif kind == "B":
            for way in (1, -1):
                arrived(RING_SENDS[slot, way])
                start(RING_PASSES[slot, way])
        else:
            for way in (1, -1):
                arrived(RING_PASSES[slot, way])
            start(CROSSES[slot, 0])

    def handle_all(*place):
        for event in EVENTS.get(place, []):
            handle(event)

    for m in (0, 1):
        for n in HOPS[0, m]:
            if COPIES[n][2] == "Q":
                start(n)
    for m in (0, 1):
        for n in HOPS[0, m]:
            if COPIES[n][2] == "P" and m == 0:
                start(n)


    def keep_top(slot):
        for lane in range(2):
            held = [top[lane, i] for i in range(K)]
            for part in range(CHUNK // 256):
                fresh = [
                    scores[slot, part * 256 + i * 8 : part * 256 + i * 8 + 8, lane * 128 : lane * 128 + 128]
                    for i in range(K)
                ]
                held = merge_down(held, sort_down(fresh))
            for i in range(K):
                top[lane, i] = held[i]

    def retrieve(i, carry):
        now = lax.rem(i, 2)
        entity_copy(i).wait()
        keep_top(1 - now)
        scores[now] = lax.dot_general(entities[i], mentions_ref[...], NT, preferred_element_type=F32)

        for place in range(chunks):
            if ("r", place) in EVENTS:

                @pl.when(i == place)
                def _(place=place):
                    handle_all("r", place)

        return carry

    lax.fori_loop(0, chunks, retrieve, 0)
    keep_top((chunks - 1) % 2)

    def list_copy(stage, way):
        axis = "PQ"[stage]
        return pltpu.make_async_remote_copy(
            src_ref=lists.at[stage], dst_ref=lists_in.at[stage, way - 1],
            send_sem=list_send.at[stage, way - 1], recv_sem=list_recv.at[stage, way - 1],
            device_id=(along(axis, way), men), device_id_type=MESH,
        )

    for lane in range(2):
        held = [top[lane, i] for i in range(K)]
        for shift in (4, 2, 1):
            held = merge_down(held, [pltpu.roll(row, shift, 0) for row in held])
        for i in range(K):
            top[lane, i] = held[i]
            lists[0, i : i + 1, lane * 128 : lane * 128 + 128] = held[i][0:1]
    for way in (1, 2, 3):
        list_copy(0, way).start()

    handle_all("m", 0)

    local[2].wait()

    def prepare(t, carry):
        part = pl.ds(pl.multiple_of(t * LEN, LEN), LEN)
        pair = (rows[part, :].astype(F32) + mention_rows[pl.ds(t, 1), :]).astype(BF16).astype(F32)
        square = jnp.mean(pair * pair, axis=1, keepdims=True)
        rows[part, :] = (pair * lax.rsqrt(square + 1e-06)).astype(BF16)
        total[part, :] = pair
        return carry

    for part in (0, 1):
        lax.fori_loop(part * 8, part * 8 + 8, prepare, 0)
        handle_all("p", part)
    local[0].wait()
    local[1].wait()

    def merge_lists(stage):
        for way in (1, 2, 3):
            list_copy(stage, way).wait_recv()
        for lane in range(2):
            span = slice(lane * 128, lane * 128 + 128)
            held = [top[lane, i] for i in range(K)]
            for way in range(3):
                held = merge_down(
                    held, [jnp.broadcast_to(lists_in[stage, way, i : i + 1, span], (8, 128)) for i in range(K)]
                )
            for i in range(K):
                if stage == 0:
                    top[lane, i] = held[i]
                    lists[1, i : i + 1, span] = held[i][0:1]
                else:
                    best_ref[i : i + 1, span] = held[i][0:1]

    for step, (low, high) in enumerate(STEPS):
        handle_all(step, 0)
        for slot in range(max(low, 1), high):
            for m in (0, 1):
                if (slot, m) in CROSSES:
                    arrived(CROSSES[slot, m])
        width = (high - low) * 256
        size = 768 if high - low < 3 else 512

        def feed(tile, carry, step=step, low=low, high=high, width=width, size=size):
            for place in (1, 2):
                if (step, place) in EVENTS:

                    @pl.when(tile == place)
                    def _(place=place):
                        handle_all(step, place)

            part = pl.ds(pl.multiple_of(tile * size, size), size)
            pre = lax.dot_general(
                rows[part, :], weights[low:high, 0].reshape(width, 1024), NT, preferred_element_type=F32
            )
            act = gelu(pre).astype(BF16)
            total[part, :] += jnp.dot(act, weights[low:high, 1].reshape(width, 1024), preferred_element_type=F32)
            return carry

        lax.fori_loop(0, rows.shape[0] // size, feed, 0)
        if step == LIST_STEP:
            merge_lists(0)
            for way in (1, 2, 3):
                list_copy(1, way).start()

    head = head_ref[...].astype(F32).reshape(1, -1)

    def score(t, carry):
        part = pl.ds(pl.multiple_of(t * LEN, LEN), LEN)
        mixed = total[part, :]
        square = jnp.mean(mixed * mixed, axis=1, keepdims=True)
        dots = jnp.sum(mixed * head, axis=1, keepdims=True)
        value = jnp.sum(dots * lax.rsqrt(square + 1e-06), axis=0, keepdims=True) * (1.0 / LEN)
        return jnp.where(slot_col == t, jnp.broadcast_to(value, (16, 128)), carry)

    pair_score = lax.fori_loop(0, 16, score, jnp.zeros((16, 128), F32))
    live = count_ref[0]
    owner = jnp.zeros((16, 128), jnp.int32)
    for t in range(16):
        owner = jnp.where(slot_col == t, owner_ref[t], owner)
    rank = jnp.zeros((16, 128), jnp.int32)
    for s in range(16):
        same = (slot_col > s) & (owner == owner_ref[s]) & (jnp.full((16, 128), s, jnp.int32) < live)
        rank = rank + jnp.where(same, 1, 0)
    lane_id = lax.broadcasted_iota(jnp.int32, (16, 128), 1)
    base = jnp.where((lane_id == men * 2 + rank) & (slot_col < live), pair_score, 0.0)
    for o in range(8):
        line = jnp.sum(jnp.where(owner == o, base, 0.0), axis=0, keepdims=True)
        placed[o] = jnp.broadcast_to(line, (8, 128))

    def place_copy(way):
        goal = lax.rem(men + way, 8)
        return pltpu.make_async_remote_copy(
            src_ref=placed.at[goal], dst_ref=placed_in.at[way - 1],
            send_sem=place_send.at[way - 1], recv_sem=place_recv.at[way - 1],
            device_id=(kb, goal), device_id_type=MESH,
        )

    for way in range(1, 8):
        place_copy(way).start()
    merge_lists(1)
    owned = placed[men]
    for n in range(len(COPIES)):
        copy_of(n).wait_send()
    for stage in (0, 1):
        for way in (1, 2, 3):
            list_copy(stage, way).wait_send()
    for way in range(1, 8):
        place_copy(way).wait()
        owned = owned + placed_in[way - 1]
    owned_ref[...] = owned


def hand_over(best_ref, owned_ref, best_out, owned_out):
    best_out[...] = best_ref[...]
    owned_out[...] = owned_ref[0:1, 0:16]


def body(mentions, kb_embed, blocks, task_mention, task_owner, task_count, w_in, w_out, head):
    width = mentions.shape[1]
    token_rows = blocks.shape[0] * blocks.shape[1]
    group = mentions.shape[0]
    anywhere = pl.BlockSpec(memory_space=pl.ANY)
    vmem = pl.BlockSpec(memory_space=pltpu.VMEM)
    smem = pl.BlockSpec(memory_space=pltpu.SMEM)
    dma = pltpu.SemaphoreType.DMA
    best, owned = pl.pallas_call(
        kernel,
        out_shape=(jax.ShapeDtypeStruct((K, group), F32), jax.ShapeDtypeStruct((8, 128), F32)),
        in_specs=[vmem, anywhere, anywhere, smem, smem, smem, anywhere, anywhere, vmem],
        out_specs=(vmem, vmem),
        scratch_shapes=[
            pltpu.VMEM((token_rows, width), BF16),
            pltpu.VMEM((token_rows, width), F32),
            pltpu.VMEM((16, 2, 256, width), BF16),
            pltpu.VMEM((kb_embed.shape[0] // CHUNK, CHUNK, width), BF16),
            pltpu.VMEM((2, CHUNK, group), F32),
            pltpu.VMEM((2, K, 8, 128), F32),
            pltpu.VMEM((16, width), F32),
            pltpu.VMEM((2, K, group), F32),
            pltpu.VMEM((2, 3, K, group), F32),
            pltpu.VMEM((8, 8, 128), F32),
            pltpu.VMEM((7, 8, 128), F32),
            dma((len(COPIES),)),
            dma((len(COPIES),)),
            dma((3,)),
            dma((kb_embed.shape[0] // CHUNK,)),
            dma((2, 3)),
            dma((2, 3)),
            dma((7,)),
            dma((7,)),
        ],
        compiler_params=pltpu.CompilerParams(
            collective_id=0, has_side_effects=True, vmem_limit_bytes=60 * 1024 * 1024
        ),
        cost_estimate=pl.CostEstimate(flops=28_000_000_000, bytes_accessed=14_000_000, transcendentals=6_300_000),
    )(
        mentions, kb_embed, blocks.reshape(token_rows, width), task_mention, task_owner.reshape(-1), task_count,
        w_in, w_out, head,
    )
    best, owned = pl.pallas_call(
        hand_over,
        out_shape=(jax.ShapeDtypeStruct(best.shape, F32), jax.ShapeDtypeStruct((1, 16), F32)),
        in_specs=[vmem, vmem],
        out_specs=(vmem, vmem),
    )(best, owned)
    return best.T, owned


def solution(mesh):
    in_specs = (
        P("men", None),
        P("kb", None),
        P(("kb", "men"), None, None),
        P(("kb", "men")),
        P(("kb", "men"), None),
        P(("kb", "men")),
        P("kb", None),
        P("kb", None),
        P(),
    )
    out_specs = (P("men", None), P(("kb", "men"), None))
    return jax.shard_map(body, mesh=mesh, in_specs=in_specs, out_specs=out_specs, check_vma=False)
```

```python
import functools

import jax
import jax.numpy as jnp
from jax import lax
from jax.experimental import pallas as pl
from jax.experimental.pallas import tpu as pltpu
from jax.sharding import PartitionSpec as P

K = 32
LEN = 96
MESH = pl.DeviceIdType.MESH
NT = (((1,), (1,)), ((), ()))
F32 = jnp.float32
BF16 = jnp.bfloat16
RING = 4

ITEMS = [
    (0, 0), (-1, 0), (1, 0), (0, -1), (0, 1), (2, 0), (0, 2), (-1, 1),
    (-1, -1), (1, 1), (1, -1), (2, 1), (-1, 2), (1, 2), (2, -1), (2, 2),
]
SLOT = {item: slot for slot, item in enumerate(ITEMS)}
QUARTERED = {SLOT[item] for item in ((0, 1), (0, -1), (0, 2),)}


def wrap(offset):
    return (offset + 1) % RING - 1


def hops(item):
    first, second = item
    if item == (0, 0):
        return [("Q", way, mat) for mat in (0, 1) for way in (1, -1)] + [
            ("P", way, mat) for mat in (0, 1) for way in (1, -1)
        ]
    out = []
    if second == 0:
        if first == -1:
            out.append(("P", 1, 0))
        if first == 1:
            out.append(("P", -1, 1))
        out += [("Q", way, mat) for mat in (0, 1) for way in (1, -1)]
    elif second == -1:
        out.append(("Q", 1, 0))
    elif second == 1:
        out.append(("Q", -1, 1))
    return out


COPIES = []
HOPS, HOPPED, RING_SENDS, RING_PASSES, CROSSES = {}, {}, {}, {}, {}
for item in ITEMS:
    slot = SLOT[item]
    for axis, way, mat in hops(item):
        goal = (wrap(item[0] - way), item[1]) if axis == "P" else (item[0], wrap(item[1] - way))
        HOPS.setdefault((slot, mat), []).append(len(COPIES))
        HOPPED[SLOT[goal], mat] = len(COPIES)
        COPIES.append(("hop", slot, axis, way, mat, SLOT[goal]))
for slot in sorted(QUARTERED):
    for way in (1, -1):
        RING_SENDS[slot, way] = len(COPIES)
        COPIES.append(("ring", slot, way, 0, 2, 0))
        RING_PASSES[slot, way] = len(COPIES)
        COPIES.append(("ring", slot, way, (1 - way) // 2, 1, -way))
    CROSSES[slot, 0] = len(COPIES)
    COPIES.append(("cross", slot, 0, 2))
for slot in range(1, 16):
    if slot not in QUARTERED:
        for mat in (0, 1):
            CROSSES[slot, mat] = len(COPIES)
            COPIES.append(("cross", slot, mat, 1))

EVENTS = {
    ("r", 0): [("L",)],
    ("r", 7): [("A", (0, -1)), ("A", (0, 1))],
    ("p", 0): [("D", (-1, 0), 0), ("D", (1, 0), 0)],
    (0, 1): [("A", (0, 2)), ("B", (0, -1))],
    (1, 0): [("D", (-1, 0), 1), ("D", (1, 0), 1), ("B", (0, 1)), ("D", (-1, 1), 0)],
    (1, 1): [("D", (-1, -1), 0), ("B", (0, 2))],
    (2, 0): [("D", (2, 0), 0), ("D", (1, 1), 0), ("C", (0, -1)), ("C", (0, 1)), ("D", (1, -1), 0), ("D", (2, 0), 1), ("C", (0, 2))],
    (2, 1): [("D", (-1, 1), 1), ("D", (-1, -1), 1)],
    (3, 0): [("D", (1, 1), 1), ("D", (1, -1), 1)],
    (3, 1): [("D", (2, 1), 0), ("D", (-1, 2), 0)],
    (4, 0): [("D", (2, -1), 0), ("D", (2, 1), 1)],
    (4, 1): [("D", (-1, 2), 1), ("D", (1, 2), 0)],
    (5, 0): [("D", (1, 2), 1), ("D", (2, -1), 1)],
    (5, 1): [("D", (2, 2), 0), ("D", (2, 2), 1)],
}


def sort_pairs(count):
    pairs = []
    p = 1
    while p < count:
        k = p
        while k >= 1:
            for j in range(k % p, count - k, 2 * k):
                for i in range(min(k, count - j - k)):
                    if (i + j) // (2 * p) == (i + j + k) // (2 * p):
                        pairs.append((i + j, i + j + k))
            k //= 2
        p *= 2
    return pairs


PAIRS = sort_pairs(K)


def sort_down(rows):
    rows = list(rows)
    for i, j in PAIRS:
        rows[i], rows[j] = jnp.maximum(rows[i], rows[j]), jnp.minimum(rows[i], rows[j])
    return rows


def merge_down(left, right):
    rows = [jnp.maximum(left[i], right[K - 1 - i]) for i in range(K)]
    stride = K // 2
    while stride:
        for i in range(K):
            if not i & stride:
                rows[i], rows[i + stride] = (
                    jnp.maximum(rows[i], rows[i + stride]),
                    jnp.minimum(rows[i], rows[i + stride]),
                )
        stride //= 2
    return rows


def gelu(x):
    half = 0.5 * x
    return half + half * lax.erf(x * 0.7071067811865476)


CHUNK = 512
LIST_STEP = 3
STEPS = [(0, 1), (1, 3), (3, 5), (5, 9), (9, 11), (11, 13), (13, 16)]


def kernel(
    mentions_ref, kb_ref, blocks_ref, pick_ref, owner_ref, count_ref, w_in_ref, w_out_ref, head_ref,
    best_ref, owned_ref,
    rows, total, values, weights, entities, scores, top, mention_rows, lists, lists_in, placed, placed_in,
    send, recv, local_sem, kb_sem, list_send, list_recv, place_send, place_recv,
):
    kb = lax.axis_index("kb")
    men = lax.axis_index("men")
    core = lax.rem(men, 2)
    z, x = kb // RING, lax.rem(kb, RING)
    partner = men + 1 - 2 * core
    layer = men // 2

    def along(axis, way):
        step = way % RING
        dz = step * (1 - core) if axis == "P" else step * core
        dx = step * core if axis == "P" else step * (1 - core)
        return lax.rem(z + dz, RING) * RING + lax.rem(x + dx, RING)

    near = {(axis, way): along(axis, way) for axis in "PQ" for way in (1, -1)}
    mine = pl.ds(pl.multiple_of(core * 128, 128), 128)
    shards = (w_in_ref, w_out_ref)

    barrier = pltpu.get_barrier_semaphore()
    for axis in "PQ":
        for way in (1, 2, 3):
            pl.semaphore_signal(barrier, inc=1, device_id=(along(axis, way), men), device_id_type=MESH)
    for way in range(1, 8):
        pl.semaphore_signal(barrier, inc=1, device_id=(kb, lax.rem(men + way, 8)), device_id_type=MESH)

    local = [pltpu.make_async_copy(shards[m], weights.at[0, m], local_sem.at[m]) for m in (0, 1)]
    local.append(pltpu.make_async_copy(blocks_ref, rows, local_sem.at[2]))

    def entity_copy(i):
        return pltpu.make_async_copy(
            kb_ref.at[pl.ds(pl.multiple_of(i * CHUNK, CHUNK), CHUNK)], entities.at[i], kb_sem.at[i]
        )

    chunks = kb_ref.shape[0] // CHUNK
    entity_copy(0).start()
    local[0].start()
    local[1].start()
    for i in range(1, chunks):
        entity_copy(i).start()
    local[2].start()

    slot_col = lax.broadcasted_iota(jnp.int32, (16, 128), 0)
    pick = jnp.zeros((16, 128), jnp.int32)
    for t in range(16):
        pick = jnp.where(slot_col == t, pick_ref[t], pick)
    one_hot = (
        jnp.concatenate([pick, pick], axis=1) == lax.broadcasted_iota(jnp.int32, (16, 256), 1)
    ).astype(F32).astype(BF16)
    mention_rows[...] = jnp.dot(one_hot, mentions_ref[...], preferred_element_type=F32)
    top[...] = jnp.full(top.shape, -jnp.inf, F32)
    scores[1] = jnp.full(scores.shape[1:], -jnp.inf, F32)

    pl.semaphore_wait(barrier, 13)

    quarters = {
        way: pl.ds(pl.multiple_of(core * 128 + lax.rem(layer + way % RING, RING) * 32, 32), 32) for way in (-1, 0, 1)
    }
    rings = {way: lax.rem(men + 2 * (way % RING), 8) for way in (1, -1)}

    def copy_of(n):
        kind, slot, *rest = COPIES[n]
        if kind == "hop":
            axis, way, m, goal = rest
            part = quarters[0] if goal in QUARTERED else mine
            source = shards[m].at[part] if slot == 0 else weights.at[slot, m, part]
            target = weights.at[goal, m, part]
            device = (near[axis, way], men)
        elif kind == "ring":
            way, m, count, shift = rest
            source = target = weights.at[slot, pl.ds(m, count), quarters[shift]]
            device = (kb, rings[way])
        else:
            m, count = rest
            source = target = weights.at[slot, pl.ds(m, count), mine]
            device = (kb, partner)
        return pltpu.make_async_remote_copy(
            src_ref=source, dst_ref=target, send_sem=send.at[n], recv_sem=recv.at[n],
            device_id=device, device_id_type=MESH,
        )

    def start(n):
        copy_of(n).start()

    def arrived(n):
        copy_of(n).wait_recv()

    def handle(event):
        if event[0] == "L":
            for n in HOPS[0, 1]:
                if COPIES[n][2] == "P":
                    start(n)
            return
        kind, item = event[:2]
        slot = SLOT[item]
        if kind == "D":
            m = event[2]
            arrived(HOPPED[slot, m])
            for n in HOPS.get((slot, m), []):
                start(n)
            start(CROSSES[slot, m])
        elif kind == "A":
            for m in (0, 1):
                arrived(HOPPED[slot, m])
                for n in HOPS.get((slot, m), []):
                    start(n)
            for way in (1, -1):
                start(RING_SENDS[slot, way])
        elif kind == "B":
            for way in (1, -1):
                arrived(RING_SENDS[slot, way])
                start(RING_PASSES[slot, way])
        else:
            for way in (1, -1):
                arrived(RING_PASSES[slot, way])
            start(CROSSES[slot, 0])

    def handle_all(*place):
        for event in EVENTS.get(place, []):
            handle(event)

    for m in (0, 1):
        for n in HOPS[0, m]:
            if COPIES[n][2] == "Q":
                start(n)
    for m in (0, 1):
        for n in HOPS[0, m]:
            if COPIES[n][2] == "P" and m == 0:
                start(n)


    def keep_top(slot):
        for lane in range(2):
            held = [top[lane, i] for i in range(K)]
            for part in range(CHUNK // 256):
                fresh = [
                    scores[slot, part * 256 + i * 8 : part * 256 + i * 8 + 8, lane * 128 : lane * 128 + 128]
                    for i in range(K)
                ]
                held = merge_down(held, sort_down(fresh))
            for i in range(K):
                top[lane, i] = held[i]

    def retrieve(i, carry):
        now = lax.rem(i, 2)
        entity_copy(i).wait()
        keep_top(1 - now)
        scores[now] = lax.dot_general(entities[i], mentions_ref[...], NT, preferred_element_type=F32)

        for place in range(chunks):
            if ("r", place) in EVENTS:

                @pl.when(i == place)
                def _(place=place):
                    handle_all("r", place)

        return carry

    lax.fori_loop(0, chunks, retrieve, 0)
    keep_top((chunks - 1) % 2)

    def list_copy(stage, way):
        axis = "PQ"[stage]
        return pltpu.make_async_remote_copy(
            src_ref=lists.at[stage], dst_ref=lists_in.at[stage, way - 1],
            send_sem=list_send.at[stage, way - 1], recv_sem=list_recv.at[stage, way - 1],
            device_id=(along(axis, way), men), device_id_type=MESH,
        )

    for lane in range(2):
        held = [top[lane, i] for i in range(K)]
        for shift in (4, 2, 1):
            held = merge_down(held, [pltpu.roll(row, shift, 0) for row in held])
        for i in range(K):
            top[lane, i] = held[i]
            lists[0, i : i + 1, lane * 128 : lane * 128 + 128] = held[i][0:1]
    for way in (1, 2, 3):
        list_copy(0, way).start()

    handle_all("m", 0)

    local[2].wait()

    def prepare(t, carry):
        part = pl.ds(pl.multiple_of(t * LEN, LEN), LEN)
        pair = (rows[part, :].astype(F32) + mention_rows[pl.ds(t, 1), :]).astype(BF16).astype(F32)
        square = jnp.mean(pair * pair, axis=1, keepdims=True)
        rows[part, :] = (pair * lax.rsqrt(square + 1e-06)).astype(BF16)
        total[part, :] = pair
        return carry

    for part in (0, 1):
        lax.fori_loop(part * 8, part * 8 + 8, prepare, 0)
        handle_all("p", part)
    local[0].wait()
    local[1].wait()

    def merge_lists(stage):
        for way in (1, 2, 3):
            list_copy(stage, way).wait_recv()
        for lane in range(2):
            span = slice(lane * 128, lane * 128 + 128)
            held = [top[lane, i] for i in range(K)]
            for way in range(3):
                held = merge_down(
                    held, [jnp.broadcast_to(lists_in[stage, way, i : i + 1, span], (8, 128)) for i in range(K)]
                )
            for i in range(K):
                if stage == 0:
                    top[lane, i] = held[i]
                    lists[1, i : i + 1, span] = held[i][0:1]
                else:
                    best_ref[i : i + 1, span] = held[i][0:1]

    head = head_ref[...].astype(F32).reshape(1, -1)

    for step, (low, high) in enumerate(STEPS):
        handle_all(step, 0)
        for slot in range(max(low, 1), high):
            for m in (0, 1):
                if (slot, m) in CROSSES:
                    arrived(CROSSES[slot, m])
        width = (high - low) * 256
        size = 768 if high - low < 3 else 512

        def feed(tile, carry, step=step, low=low, high=high, width=width, size=size):
            for place in (1, 2):
                if (step, place) in EVENTS:

                    @pl.when(tile == place)
                    def _(place=place):
                        handle_all(step, place)

            part = pl.ds(pl.multiple_of(tile * size, size), size)
            pre = lax.dot_general(
                rows[part, :], weights[low:high, 0].reshape(width, 1024), NT, preferred_element_type=F32
            )
            act = gelu(pre).astype(BF16)
            mixed = total[part, :] + jnp.dot(
                act, weights[low:high, 1].reshape(width, 1024), preferred_element_type=F32
            )
            if high == len(ITEMS):
                square = jnp.mean(mixed * mixed, axis=1, keepdims=True)
                dots = jnp.sum(mixed * head, axis=1, keepdims=True)
                values[part, :] = jnp.broadcast_to(dots * lax.rsqrt(square + 1e-06), (size, 128))
            else:
                total[part, :] = mixed
            return carry

        lax.fori_loop(0, rows.shape[0] // size, feed, 0)
        if step == LIST_STEP:
            merge_lists(0)
            for way in (1, 2, 3):
                list_copy(1, way).start()

    pair_score = jnp.zeros((16, 128), F32)
    for t in range(16):
        value = jnp.sum(values[t * LEN : t * LEN + LEN, :], axis=0, keepdims=True) * (1.0 / LEN)
        pair_score = jnp.where(slot_col == t, jnp.broadcast_to(value, (16, 128)), pair_score)
    live = count_ref[0]
    owner = jnp.zeros((16, 128), jnp.int32)
    for t in range(16):
        owner = jnp.where(slot_col == t, owner_ref[t], owner)
    rank = jnp.zeros((16, 128), jnp.int32)
    for s in range(16):
        same = (slot_col > s) & (owner == owner_ref[s]) & (jnp.full((16, 128), s, jnp.int32) < live)
        rank = rank + jnp.where(same, 1, 0)
    lane_id = lax.broadcasted_iota(jnp.int32, (16, 128), 1)
    base = jnp.where((lane_id == men * 2 + rank) & (slot_col < live), pair_score, 0.0)
    for o in range(8):
        line = jnp.sum(jnp.where(owner == o, base, 0.0), axis=0, keepdims=True)
        placed[o] = jnp.broadcast_to(line, (8, 128))

    def place_copy(way):
        goal = lax.rem(men + way, 8)
        return pltpu.make_async_remote_copy(
            src_ref=placed.at[goal], dst_ref=placed_in.at[way - 1],
            send_sem=place_send.at[way - 1], recv_sem=place_recv.at[way - 1],
            device_id=(kb, goal), device_id_type=MESH,
        )

    for way in range(1, 8):
        place_copy(way).start()
    merge_lists(1)
    owned = placed[men]
    for n in range(len(COPIES)):
        copy_of(n).wait_send()
    for stage in (0, 1):
        for way in (1, 2, 3):
            list_copy(stage, way).wait_send()
    for way in range(1, 8):
        place_copy(way).wait()
        owned = owned + placed_in[way - 1]
    owned_ref[...] = owned


def hand_over(best_ref, owned_ref, best_out, owned_out):
    best_out[...] = best_ref[...]
    owned_out[...] = owned_ref[0:1, 0:16]


def body(mentions, kb_embed, blocks, task_mention, task_owner, task_count, w_in, w_out, head):
    width = mentions.shape[1]
    token_rows = blocks.shape[0] * blocks.shape[1]
    group = mentions.shape[0]
    anywhere = pl.BlockSpec(memory_space=pl.ANY)
    vmem = pl.BlockSpec(memory_space=pltpu.VMEM)
    smem = pl.BlockSpec(memory_space=pltpu.SMEM)
    dma = pltpu.SemaphoreType.DMA
    best, owned = pl.pallas_call(
        kernel,
        out_shape=(jax.ShapeDtypeStruct((K, group), F32), jax.ShapeDtypeStruct((8, 128), F32)),
        in_specs=[vmem, anywhere, anywhere, smem, smem, smem, anywhere, anywhere, vmem],
        out_specs=(vmem, vmem),
        scratch_shapes=[
            pltpu.VMEM((token_rows, width), BF16),
            pltpu.VMEM((token_rows, width), F32),
            pltpu.VMEM((token_rows, 128), F32),
            pltpu.VMEM((16, 2, 256, width), BF16),
            pltpu.VMEM((kb_embed.shape[0] // CHUNK, CHUNK, width), BF16),
            pltpu.VMEM((2, CHUNK, group), F32),
            pltpu.VMEM((2, K, 8, 128), F32),
            pltpu.VMEM((16, width), F32),
            pltpu.VMEM((2, K, group), F32),
            pltpu.VMEM((2, 3, K, group), F32),
            pltpu.VMEM((8, 8, 128), F32),
            pltpu.VMEM((7, 8, 128), F32),
            dma((len(COPIES),)),
            dma((len(COPIES),)),
            dma((3,)),
            dma((kb_embed.shape[0] // CHUNK,)),
            dma((2, 3)),
            dma((2, 3)),
            dma((7,)),
            dma((7,)),
        ],
        compiler_params=pltpu.CompilerParams(
            collective_id=0, has_side_effects=True, vmem_limit_bytes=60 * 1024 * 1024
        ),
        cost_estimate=pl.CostEstimate(flops=28_000_000_000, bytes_accessed=14_000_000, transcendentals=6_300_000),
    )(
        mentions, kb_embed, blocks.reshape(token_rows, width), task_mention, task_owner.reshape(-1), task_count,
        w_in, w_out, head,
    )
    best, owned = pl.pallas_call(
        hand_over,
        out_shape=(jax.ShapeDtypeStruct(best.shape, F32), jax.ShapeDtypeStruct((1, 16), F32)),
        in_specs=[vmem, vmem],
        out_specs=(vmem, vmem),
    )(best, owned)
    return best.T, owned


def solution(mesh):
    in_specs = (
        P("men", None),
        P("kb", None),
        P(("kb", "men"), None, None),
        P(("kb", "men")),
        P(("kb", "men"), None),
        P(("kb", "men")),
        P("kb", None),
        P("kb", None),
        P(),
    )
    out_specs = (P("men", None), P(("kb", "men"), None))
    return jax.shard_map(body, mesh=mesh, in_specs=in_specs, out_specs=out_specs, check_vma=False)
```
